1024 devices in a mesh: dp: 64 (over z, core), expert: 16 (over y, x).
Axes of the slice: x: 4, y: 4, z: 32, core: 2. Of those that a mesh axis runs over, the one named last changes fastest.
Arguments:
- out_grad: bfloat16 [131072, 3584], P(('dp', 'expert')), may hold values from -0.29882812 to 0.29882812
- router_input: bfloat16 [131072, 3584], P(('dp', 'expert')), may hold values from -24 to 24
- down_weight: bfloat16 [16, 1024, 3584], P('expert'), may hold values from -0.1875 to 0.1875
- saved_hidden: bfloat16 [64, 16, 16, 10, 1024], P('dp', 'expert'), may hold values from -3 to 3
- expert_ids: int32 [131072, 1], P(('dp', 'expert')), may hold values from 0 to 15; in each aligned block of 128 rows (0 to 127, 128 to 255, ...) at most 10 rows name the same one
- affinity: float32 [131072, 8], P(('dp', 'expert')), may hold values from 0.05 to 0.95
- other_dgate: float32 [131072, 7], P(('dp', 'expert')), may hold values from -6 to 6
Outputs:
- grad_hidden: bfloat16 [64, 16, 16, 10, 1024], P('dp', 'expert')
- grad_logit: float32 [131072, 8], P(('dp', 'expert'))
- grad_centroid: float32 [16, 3584], P('expert', 'dp')
The draws below stay inside these ranges and needn't reach their ends.
Inputs may be any that keep to these rules, and one draw needn't show every extreme that they name: `expert_ids`: of the 128 tokens of one device, at most 10 name the same expert, and in every draw some expert is named by exactly 10 tokens of one device.
All inputs are finite; a program needn't handle non-finite values.
Results may differ from the reference program's by a relative error of at most 0.0049.
Values may be sent and summed in bfloat16 or wider, within the bound.
A program may use at most 32 MiB of HBM per device.

```python
import math
import jax
import jax.numpy as jnp
import numpy as np
from jax import lax

D = 3584
FF = 1024
TOP = 8
TOK_DEV = 128
EXPERTS = 16
CAP = 10
TOKENS = 131072
N_DP = 64
N_EXPERT = 16


def strengthened(result, key, source, target, parts, factor):
    owner, partner = [(jnp.arange(result.shape[dim]) // (result.shape[dim] // parts)).reshape([-1 if axis == dim else 1 for axis in range(result.ndim)]) for dim in (source, target)]
    chosen = jax.random.permutation(key, parts)[partner]
    strong = (owner == chosen) | (owner == (partner + parts // 2) % parts)
    return jnp.where(strong, factor * result, result)


def level_of(key, extent, cuts, smallest, top_value):
    factor_of = 1.0
    for dim, shards_of in cuts:
        heights = jax.random.uniform(jax.random.fold_in(jax.random.fold_in(key, 6), dim), (shards_of,), jnp.float32, smallest / len(cuts), top_value / len(cuts))
        factor_of = factor_of * jnp.repeat(jnp.exp(heights), extent[dim] // shards_of).reshape((-1,) + (1,) * (len(extent) - 1 - dim))
    return factor_of


def routed_block(own_key, own, number, rows, number_of, top, bound, skew):
    order = jax.random.permutation(own_key, number_of)
    packed, usual = load_shares(number_of, rows * top, bound, skew, True), load_shares(number_of, rows * top, bound, skew, False)
    places = jnp.arange(number_of)

    def named(tallies, turn):
        used = int((tallies > 0).sum())
        fixed = max(1, used // 4)
        passed = fixed + (places - fixed + turn * (used - fixed)) % max(1, number_of - fixed)
        return jnp.zeros((number_of,), jnp.int32).at[order[jnp.where(places < fixed, places, passed)]].set(jnp.asarray(tallies, jnp.int32))

    tallies = jnp.where(number % 4 == 0, named(packed, number // 4), named(usual, number - number // 4 - 1))
    mixed = jax.random.permutation(jax.random.fold_in(own, 3), number_of)
    source_of, receiver = mixed[0:number_of // 2 * 2:2], mixed[1:number_of // 2 * 2:2]
    slack = jnp.minimum(tallies[source_of] - 1, bound - tallies[receiver]) // 2
    slack = jnp.where((source_of == order[0]) | (receiver == order[0]) | (tallies[receiver] == 0), 0, jnp.maximum(slack, 0))
    passed = jax.random.randint(jax.random.fold_in(own, 4), (number_of // 2,), 0, 1 << 20) % (slack + 1)
    tallies = tallies.at[source_of].add(-passed).at[receiver].add(passed)
    members = jnp.searchsorted(jnp.cumsum(tallies), jnp.arange(rows * top), side="right").astype(jnp.int32)
    table = members.reshape(top, rows).T
    table = table[jax.random.permutation(jax.random.fold_in(own, 1), rows)]
    turn = jax.random.randint(jax.random.fold_in(own, 2), (rows, 1), 0, top)
    return jnp.take_along_axis(table, (jnp.arange(top)[None, :] + turn) % top, axis=1)


def load_shares(count, total, reach, skew, full):
    loads = [(1 << 20) // math.isqrt(standing ** skew) + 1 for standing in range(1, count + 1)]
    largest = reach if full else min(reach, max(-(-total // count), total * loads[0] // sum(loads)))
    least = 1 if total - largest >= count - 1 else 0
    given, spare = [largest] + [least] * (count - 1), total - largest - least * (count - 1)
    while spare > 0:
        free = [i for i in range(1, count) if given[i] < largest] or [i for i in range(1, count) if given[i] < reach]
        mass, left = sum([loads[i] for i in free]), spare
        for i in free:
            addition = min(reach - given[i], max(1, left * loads[i] // mass), spare)
            given[i] = given[i] + addition
            spare = spare - addition
    return np.array(given)


def scatter_about(rng, dims, scale, bound, cuts=(), held_as=jnp.bfloat16):
    drawn = scale * jax.random.normal(rng, dims, jnp.float32)
    if cuts:
        drawn = drawn * level_of(rng, dims, cuts, -0.22, 0.18)
    return jnp.clip(drawn, -bound, bound).astype(held_as)


def gaussian_with(stream_key, dims, scale, most, split, heavy, held_as=jnp.bfloat16):
    drawn = scale * jax.random.normal(stream_key, dims, jnp.float32)
    if split:
        drawn = drawn * level_of(stream_key, dims, split, -0.22, 0.18)
    return jnp.clip(strengthened(drawn, jax.random.fold_in(stream_key, 3), *heavy), -most, most).astype(held_as)


def setup_inputs(seed: int = 0) -> dict:
    streams_of = jax.random.split(jax.random.key(seed), 8)
    out_grad = scatter_about(streams_of[0], (TOKENS, D), 0.05, 0.29882812, ((0, 1024),))
    router_input = gaussian_with(streams_of[1], (TOKENS, D), 1.0, 24.0, ((0, 1024),), (0, 1, 512, 6.0))
    down_weight = scatter_about(streams_of[2], (EXPERTS, FF, D), FF ** -0.5, 0.1875, ((0, 16),))
    saved_hidden = scatter_about(streams_of[3], (N_DP, EXPERTS, N_EXPERT, CAP, FF), 0.5, 3.0, ((0, 64), (1, 16)))
    expert_ids_keys = jax.random.split(jax.random.fold_in(streams_of[4], 1), TOKENS // TOK_DEV)
    expert_ids_turns = jax.random.permutation(jax.random.fold_in(streams_of[4], 3), TOKENS // TOK_DEV)
    expert_ids = jax.vmap(lambda own, number: routed_block(jax.random.fold_in(streams_of[4], 2), own, number, TOK_DEV, EXPERTS, 1, CAP, 2))(expert_ids_keys, expert_ids_turns).reshape((TOKENS, 1))
    affinity = jnp.clip(0.05 + 0.9 * jax.random.uniform(streams_of[5], (TOKENS, TOP), jnp.float32) ** level_of(streams_of[5], (TOKENS, TOP), ((0, 1024),), -0.2, 0.2), 0.05, 0.95)
    other_dgate = scatter_about(streams_of[6], (TOKENS, TOP - 1), 1.0, 6.0, ((0, 1024),), jnp.float32)
    return dict(out_grad=out_grad, router_input=router_input, down_weight=down_weight, saved_hidden=saved_hidden, expert_ids=expert_ids, affinity=affinity, other_dgate=other_dgate)


route_scale = 2.5


def reference(out_grad, router_input, down_weight, saved_hidden, expert_ids, affinity, other_dgate):
    sources = N_DP * N_EXPERT
    owner_col = expert_ids[:, 0].reshape(sources, TOK_DEV)
    routed = (owner_col[:, :, None] == jnp.arange(EXPERTS, dtype=jnp.int32)[None, None, :]).astype(jnp.int32)
    earlier = (jnp.cumsum(routed, axis=1).astype(jnp.int32) - routed) * routed
    slot_index = jnp.sum(earlier, axis=2).astype(jnp.int32)
    device_ids = jnp.arange(sources, dtype=jnp.int32)[:, None] + jnp.zeros((1, TOK_DEV), jnp.int32)
    dp_index = (device_ids // N_EXPERT).reshape(-1)
    src_index = (device_ids % N_EXPERT).reshape(-1)
    where_to = (dp_index, owner_col.reshape(-1), src_index, slot_index.reshape(-1))
    total_aff = jnp.sum(affinity, axis=1)
    gate_value = (route_scale * affinity[:, 0] / total_aff).astype(jnp.bfloat16)
    dispatched = jnp.zeros((N_DP, EXPERTS, N_EXPERT, CAP, D), jnp.bfloat16).at[where_to].set(out_grad)
    gate_slots = jnp.zeros((N_DP, EXPERTS, N_EXPERT, CAP), jnp.bfloat16).at[where_to].set(gate_value)

    def per_expert(items):
        rows, weight, hidden, gates = items
        grad_rows = lax.dot_general(rows.reshape(-1, D), weight, (((1,), (1,)), ((), ())), preferred_element_type=jnp.float32)
        flat_hidden = hidden.reshape(-1, FF)
        slot_dgate = jnp.sum(flat_hidden.astype(jnp.float32) * grad_rows, axis=1)
        grad_part = (gates.reshape(-1).astype(jnp.float32)[:, None] * grad_rows).astype(jnp.bfloat16)
        return slot_dgate.reshape(gates.shape), grad_part.reshape(hidden.shape)

    slot_dgate, grad_hidden = lax.map(per_expert, (jnp.swapaxes(dispatched, 0, 1), down_weight, jnp.swapaxes(saved_hidden, 0, 1), jnp.swapaxes(gate_slots, 0, 1)))
    slot_dgate = jnp.swapaxes(slot_dgate, 0, 1)
    grad_hidden = jnp.swapaxes(grad_hidden, 0, 1)
    own_dgate = slot_dgate[where_to]
    dgate = jnp.concatenate([own_dgate[:, None], other_dgate], axis=1)
    weighted = jnp.sum(dgate * affinity, axis=1) / total_aff
    grad_logit = route_scale / total_aff[:, None] * (dgate - weighted[:, None]) * affinity * (1.0 - affinity)
    chosen = expert_ids[:, 0:1] == jnp.arange(EXPERTS, dtype=jnp.int32)[None, :]
    picked = jnp.where(chosen, grad_logit[:, 0:1].astype(jnp.bfloat16), jnp.zeros((), jnp.bfloat16))
    grad_centroid = jnp.dot(picked.T, router_input, preferred_element_type=jnp.float32)
    return grad_hidden, grad_logit, grad_centroid
```

```python
import jax
import jax.numpy as jnp
from jax import lax
from jax.experimental import pallas as pl
from jax.experimental.pallas import tpu as pltpu
from jax.sharding import PartitionSpec as P

MESH = pl.DeviceIdType.MESH
ROUTE_SCALE = 2.5
BF = jnp.bfloat16
F32 = jnp.float32
I32 = jnp.int32

SIDE = 4
E = SIDE * SIDE
CAP = 10
HEAD = 8
TOK = 128
D = 3584
FF = 1024
CW = 512
NC = D // CW
BW = CW + CW // 4
ROWS = 2 * E * HEAD
NZ = 32
OUT = 56
HALF = 64

_HOP = (0, 1, 2, 1)
_ORDER = sorted(
    [(dx, dy) for dy in range(SIDE) for dx in range(SIDE) if (dx, dy) != (0, 0)],
    key=lambda o: -(_HOP[o[0]] + _HOP[o[1]]),
)
_DX = sum(o[0] * SIDE**i for i, o in enumerate(_ORDER))
_DY = sum(o[1] * SIDE**i for i, o in enumerate(_ORDER))


def dot(a, b):
    return jnp.dot(a, b, preferred_element_type=F32)


def dot_t(a, b):
    return lax.dot_general(a, b, (((1,), (1,)), ((), ())), preferred_element_type=F32)


def iota(shape, dim):
    return lax.broadcasted_iota(I32, shape, dim)


def slot_row(i):
    j = i - E * HEAD
    main = (i % HEAD) * E + i // HEAD
    rest = (HEAD + j % 2) * E + j // HEAD
    return jnp.where(i < E * HEAD, main, rest)


def kernel(
    og_h, ri_h, w_h, hid_h, ids_h, aff_h, oth_h,
    gh_o, gl_o, gc_o,
    wv, ogv, riv, hidv, idv, affv, othv,
    hp, sel, gsum, acc, vs, vr, gs, gr, xp, p1s, p1r, zs, zr,
    wsem, lsem, vsend, vrecv, osend, orecv, s1, r1, s2, r2, up, down,
):
    dp = lax.axis_index("dp")
    me = lax.axis_index("expert")
    z, core = dp // 2, dp % 2
    x, y = me % SIDE, me // SIDE

    def at(dx, dy):
        return ((y + dy) % SIDE) * SIDE + (x + dx) % SIDE

    def level(dz):
        return ((z + dz) % NZ) * 2 + core

    def around(body):
        def step(i, c):
            cx, cy = c
            body(at(cx % SIDE, cy % SIDE))
            return cx // SIDE, cy // SIDE

        lax.fori_loop(0, E - 1, step, (jnp.int32(_DX), jnp.int32(_DY)))

    small = [
        pltpu.make_async_copy(s, d, lsem.at[i])
        for i, (s, d) in enumerate(((ids_h, idv), (aff_h, affv), (oth_h, othv), (hid_h, hidv), (ri_h, riv)))
    ]
    for copy in small[:4]:
        copy.start()

    def w_copy(c):
        return pltpu.make_async_copy(w_h.at[:, pl.ds(c * CW, CW)], wv.at[c], wsem.at[c])

    def og_copy(c):
        return pltpu.make_async_copy(og_h.at[:, pl.ds(c * CW, CW)], ogv.at[c], wsem.at[NC + c])

    for c in range(NC):
        w_copy(c).start()

    barrier = pltpu.get_barrier_semaphore()

    def greet(e):
        pl.semaphore_signal(barrier, inc=1, device_id=(dp, e), device_id_type=MESH)
        pl.semaphore_signal(barrier, inc=1, device_id=(z * 2 + 1 - core, e), device_id_type=MESH)

    around(greet)
    pl.semaphore_signal(barrier, inc=1, device_id=(z * 2 + 1 - core, me), device_id_type=MESH)
    for dz in (1, NZ - 1):
        pl.semaphore_signal(barrier, inc=1, device_id=(level(dz), me), device_id_type=MESH)

    for c in range(NC):
        og_copy(c).start()
    small[4].start()

    small[3].wait()
    place = slot_row(iota((ROWS, E * CAP), 0)) == iota((ROWS, E * CAP), 1)
    hp[...] = dot(place.astype(F32).astype(BF), hidv[...]).astype(BF)

    fold = (iota((E * HEAD, CW // 4), 0) % HEAD) // 2

    def put(buf, c, p):
        buf[c, :, :, 0:CW] = p[0 : E * HEAD].reshape(E, HEAD, CW).astype(BF)
        rest = p[E * HEAD :, 0 : CW // 4]
        for q in range(1, 4):
            rest = jnp.where(fold == q, p[E * HEAD :, q * (CW // 4) : (q + 1) * (CW // 4)], rest)
        buf[c, :, :, CW:BW] = rest.reshape(E, HEAD, CW // 4).astype(BF)

    def get(buf, c):
        main = buf[c, :, :, 0:CW].astype(F32).reshape(E * HEAD, CW).astype(BF)
        rest = buf[c, :, :, CW:BW].astype(F32).reshape(E * HEAD, CW // 4)
        rest = jnp.concatenate([jnp.where(fold == q, rest, 0.0) for q in range(4)], axis=1).astype(BF)
        return jnp.concatenate([main, rest], axis=0)

    def own_block(src, dst, c):
        dst[c, me] = src[c, me]

    def send(src, dst, ssem, rsem, c):
        def one(e):
            pltpu.make_async_remote_copy(
                src_ref=src.at[c, e], dst_ref=dst.at[c, me], send_sem=ssem, recv_sem=rsem.at[c],
                device_id=(dp, e), device_id_type=MESH,
            ).start()

        around(one)

    def arrived(buf, rsem, c):
        part = buf.at[c, pl.ds(0, E - 1)]
        pltpu.make_async_copy(part, part, rsem.at[c]).wait()

    def sent(buf, ssem):
        part = buf.at[:, pl.ds(0, E - 1)]
        pltpu.make_async_copy(part, part, ssem).wait()

    def make_v(c):
        w_copy(c).wait()
        put(vs, c, dot(hp[...], wv[c]))
        own_block(vs, vr, c)

    make_v(0)
    pl.semaphore_wait(barrier, 2 * (E - 1) + 3)
    send(vs, vr, vsend, vrecv, 0)

    @pl.loop(1, NC)
    def _(c):
        make_v(c)
        send(vs, vr, vsend, vrecv, c)

    def tell(i):
        r = 2**i
        pl.semaphore_signal(up.at[i], inc=1, device_id=(level(r), me), device_id_type=MESH)
        pl.semaphore_signal(down.at[i], inc=1, device_id=(level(NZ - r), me), device_id_type=MESH)

    def hear(i):
        pl.semaphore_wait(up.at[i], 1)
        pl.semaphore_wait(down.at[i], 1)

    tell(0)

    for i in range(3):
        small[i].wait()
    ids = idv[...]
    aff = affv[...]
    routed = (iota((E, TOK), 0) == ids).astype(F32)
    before = (iota((TOK, TOK), 0) < iota((TOK, TOK), 1)).astype(F32).astype(BF)
    earlier = dot(routed.astype(BF), before)
    slot = jnp.sum(routed * earlier, axis=0, keepdims=True)
    wanted = slot * float(E) + ids.astype(F32)
    mine = slot_row(iota((ROWS, TOK), 0)).astype(F32) == wanted
    sel[...] = mine.astype(F32)
    total = jnp.sum(aff, axis=0, keepdims=True)
    gate = (ROUTE_SCALE * aff[0:1] / total).astype(BF).astype(F32)

    small[4].wait()
    for j in range(NZ // 2):
        start = 4 * OUT * j
        low = start // 128 * 128
        off = start - low
        width = min(384, D - low) if off + 4 * OUT > 256 else 256
        lane = iota((width, 256), 1)
        source = (2 * ((lane % 128) // HALF) + lane // 128) * OUT + lane % HALF + off
        hot = (iota((width, 256), 0) == source) & (lane % HALF < OUT)
        moved = dot(riv[:, low : low + width], hot.astype(F32).astype(BF)).astype(BF)
        q, h = j // 2, j % 2
        xp[q * TOK : (q + 1) * TOK, h * 128 : (h + 1) * 128] = moved[:, 0:128]
        xp[q * TOK : (q + 1) * TOK, 256 + h * 128 : 256 + (h + 1) * 128] = moved[:, 128:256]

    hear(0)
    tell(1)

    scaled = (sel[...] * gate).astype(BF)

    @pl.loop(0, NC)
    def _(c):
        og_copy(c).wait()
        put(gs, c, dot(scaled, ogv[c]))
        own_block(gs, gr, c)

    hear(1)
    tell(2)

    gsum[...] = jnp.zeros_like(gsum)

    @pl.loop(0, NC)
    def _(c):
        arrived(vr, vrecv, c)
        gsum[...] += dot_t(get(vr, c), ogv[c])

    own = jnp.sum(gsum[...] * sel[...], axis=0, keepdims=True)
    dgate = jnp.concatenate([own, othv[...]], axis=0)
    weighted = jnp.sum(dgate * aff, axis=0, keepdims=True) / total
    grad_logit = ROUTE_SCALE / total * (dgate - weighted) * aff * (1.0 - aff)
    gl_o[...] = grad_logit

    rows = iota((E * 8, TOK), 0)
    picked = jnp.where((rows // 8) == ids, grad_logit[0:1].astype(BF).astype(F32), 0.0)
    wide = jnp.concatenate([jnp.where(rows % 8 == q, picked, 0.0).astype(BF) for q in range(8)], axis=1)
    term = dot(wide, xp[...]).reshape(E, 8, 512).astype(BF)
    p1s[0] = term[:, :, 0:256]
    p1s[1] = term[:, :, 256:512]
    index = core * E + me
    p1r[index] = p1s[core, me]

    def term_to(e, k):
        pltpu.make_async_remote_copy(
            src_ref=p1s.at[k, e], dst_ref=p1r.at[index], send_sem=s1, recv_sem=r1,
            device_id=(z * 2 + k, e), device_id_type=MESH,
        ).start()

    def term_both(e):
        term_to(e, core)
        term_to(e, 1 - core)

    around(term_both)
    term_to(me, 1 - core)

    hear(2)
    tell(3)

    part = p1r.at[pl.ds(0, 2 * E - 1)]
    pltpu.make_async_copy(part, part, r1).wait()
    plane = jnp.sum(p1r[...].astype(F32), axis=0)
    for q in range(8):
        for h in range(2):
            zs[2 * q + h] = plane[q : q + 1, h * 128 : (h + 1) * 128]
    zr[z] = zs[z // 2]

    hear(3)

    @pl.loop(0, NZ - 1)
    def _(i):
        k = (i + 1) // 2
        dz = NZ // 2 + k * (1 - 2 * (i % 2))
        to = (z + dz) % NZ
        pltpu.make_async_remote_copy(
            src_ref=zs.at[to // 2], dst_ref=zr.at[z], send_sem=s2, recv_sem=r2,
            device_id=(to * 2 + core, me), device_id_type=MESH,
        ).start()

    @pl.loop(0, NC)
    def _(c):
        send(gs, gr, osend, orecv, c)

    acc[...] = jnp.zeros_like(acc)

    @pl.loop(0, NC)
    def _(c):
        arrived(gr, orecv, c)
        acc[...] += dot_t(get(gr, c), wv[c])

    back = (slot_row(iota((E * CAP, ROWS), 1)) == iota((E * CAP, ROWS), 0)).astype(F32).astype(BF)
    high = acc[...].astype(BF)
    low = (acc[...] - high.astype(F32)).astype(BF)
    gh_o[...] = (dot(back, high) + dot(back, low)).astype(BF)

    part = zr.at[pl.ds(0, NZ - 1)]
    pltpu.make_async_copy(part, part, r2).wait()
    column = zr[0]
    for i in range(1, NZ):
        column = column + zr[i]
    gc_o[...] = jnp.where(z % 2 == 0, column[:, 0:OUT], column[:, HALF : HALF + OUT])

    sent(vs, vsend)
    sent(gs, osend)
    part = p1r.at[pl.ds(0, 2 * E - 1)]
    pltpu.make_async_copy(part, part, s1).wait()
    part = zr.at[pl.ds(0, NZ - 1)]
    pltpu.make_async_copy(part, part, s2).wait()


def body(out_grad, router_input, down_weight, saved_hidden, expert_ids, affinity, other_dgate):
    hidden = saved_hidden[0, 0].transpose(1, 0, 2).reshape(CAP * E, FF)
    vmem, dma = pltpu.VMEM, pltpu.SemaphoreType.DMA
    hbm = pl.BlockSpec(memory_space=pl.ANY)
    here = pl.BlockSpec(memory_space=pltpu.VMEM)
    block = (NC, E, HEAD, BW)
    grad_hidden, grad_logit, grad_centroid = pl.pallas_call(
        kernel,
        out_shape=(
            jax.ShapeDtypeStruct((CAP * E, FF), BF),
            jax.ShapeDtypeStruct((8, TOK), F32),
            jax.ShapeDtypeStruct((1, OUT), F32),
        ),
        in_specs=[hbm] * 7,
        out_specs=(here, here, here),
        scratch_shapes=[
            vmem((NC, FF, CW), BF), vmem((NC, TOK, CW), BF), vmem((TOK, D), BF), vmem((CAP * E, FF), BF),
            vmem((1, TOK), I32), vmem((8, TOK), F32), vmem((7, TOK), F32),
            vmem((ROWS, FF), BF), vmem((ROWS, TOK), F32), vmem((ROWS, TOK), F32), vmem((ROWS, FF), F32),
            vmem(block, BF), vmem(block, BF), vmem(block, BF), vmem(block, BF),
            vmem((8 * TOK, 512), BF),
            vmem((2, E, 8, 256), BF), vmem((2 * E, 8, 256), BF),
            vmem((NZ // 2, 1, 128), F32), vmem((NZ, 1, 128), F32),
            dma((2 * NC,)), dma((5,)), dma, dma((NC,)), dma, dma((NC,)), dma, dma, dma, dma,
            pltpu.SemaphoreType.REGULAR((4,)), pltpu.SemaphoreType.REGULAR((4,)),
        ],
        compiler_params=pltpu.CompilerParams(
            collective_id=0, has_side_effects=True, vmem_limit_bytes=56 * 1024 * 1024
        ),
    )(out_grad, router_input, down_weight[0], hidden, expert_ids.T, affinity.T, other_dgate.T)
    grad_hidden = grad_hidden.reshape(CAP, E, FF).transpose(1, 0, 2)[None, None]
    return grad_hidden, grad_logit.T, grad_centroid


def solution(mesh):
    tokens = P(("dp", "expert"), None)
    slots = P("dp", "expert", None, None, None)
    return jax.shard_map(
        body,
        mesh=mesh,
        in_specs=(tokens, tokens, P("expert", None, None), slots, tokens, tokens, tokens),
        out_specs=(slots, tokens, P("expert", "dp")),
        check_vma=False,
    )
```

```python
import jax
import jax.numpy as jnp
from jax import lax
from jax.experimental import pallas as pl
from jax.experimental.pallas import tpu as pltpu
from jax.sharding import PartitionSpec as P

MESH = pl.DeviceIdType.MESH
ROUTE_SCALE = 2.5
BF = jnp.bfloat16
F32 = jnp.float32
I32 = jnp.int32

SIDE = 4
E = SIDE * SIDE
CAP = 10
HEAD = 8
TOK = 128
D = 3584
FF = 1024
CW = 512
NC = D // CW
BW = CW + CW // 4
ROWS = 2 * E * HEAD
NZ = 32
OUT = 56
HALF = 64
EARLY = 2

_HOP = (0, 1, 2, 1)
_ORDER = sorted(
    [(dx, dy) for dy in range(SIDE) for dx in range(SIDE) if (dx, dy) != (0, 0)],
    key=lambda o: -(_HOP[o[0]] + _HOP[o[1]]),
)


def dot(a, b):
    return jnp.dot(a, b, preferred_element_type=F32)


def dot_t(a, b):
    return lax.dot_general(a, b, (((1,), (1,)), ((), ())), preferred_element_type=F32)


def iota(shape, dim):
    return lax.broadcasted_iota(I32, shape, dim)


def slot_row(i):
    j = i - E * HEAD
    main = (i % HEAD) * E + i // HEAD
    rest = (HEAD + j % 2) * E + j // HEAD
    return jnp.where(i < E * HEAD, main, rest)


def kernel(
    og_h, ri_h, w_h, hid_h, ids_h, aff_h, oth_h,
    gh_o, gl_o, gc_o,
    wv, ogv, riv, hidv, idv, affv, othv,
    hp, sel, gsum, acc, vs, vr, gs, gr, xp, p1s, p1r, zs, zr,
    wsem, lsem, vsend, vrecv, osend, orecv, s1, r1, s2, r2, up, down,
):
    dp = lax.axis_index("dp")
    me = lax.axis_index("expert")
    z, core = lax.div(dp, 2), lax.rem(dp, 2)
    x, y = lax.rem(me, SIDE), lax.div(me, SIDE)

    def at(dx, dy):
        return lax.rem(y + dy, SIDE) * SIDE + lax.rem(x + dx, SIDE)

    def level(dz):
        return lax.rem(z + dz, NZ) * 2 + core

    others = [at(dx, dy) for dx, dy in _ORDER]

    def around(body):
        for e in others:
            body(e)

    small = [
        pltpu.make_async_copy(s, d, lsem.at[i])
        for i, (s, d) in enumerate(((ids_h, idv), (aff_h, affv), (oth_h, othv), (hid_h, hidv), (ri_h, riv)))
    ]
    for copy in small[:4]:
        copy.start()

    def w_copy(c):
        return pltpu.make_async_copy(w_h.at[:, pl.ds(c * CW, CW)], wv.at[c], wsem.at[c])

    def og_copy(c):
        return pltpu.make_async_copy(og_h.at[:, pl.ds(c * CW, CW)], ogv.at[c], wsem.at[NC + c])

    for c in range(NC):
        w_copy(c).start()

    barrier = pltpu.get_barrier_semaphore()

    def greet(e):
        pl.semaphore_signal(barrier, inc=1, device_id=(dp, e), device_id_type=MESH)
        pl.semaphore_signal(barrier, inc=1, device_id=(z * 2 + 1 - core, e), device_id_type=MESH)

    around(greet)
    pl.semaphore_signal(barrier, inc=1, device_id=(z * 2 + 1 - core, me), device_id_type=MESH)
    for dz in (1, NZ - 1):
        pl.semaphore_signal(barrier, inc=1, device_id=(level(dz), me), device_id_type=MESH)

    for c in range(NC):
        og_copy(c).start()
    small[4].start()

    small[3].wait()
    place = slot_row(iota((ROWS, E * CAP), 0)) == iota((ROWS, E * CAP), 1)
    hp[...] = dot(place.astype(F32).astype(BF), hidv[...]).astype(BF)

    fold = (iota((E * HEAD, CW // 4), 0) % HEAD) // 2

    def put(buf, c, p):
        buf[c, :, :, 0:CW] = p[0 : E * HEAD].reshape(E, HEAD, CW).astype(BF)
        rest = p[E * HEAD :, 0 : CW // 4]
        for q in range(1, 4):
            rest = jnp.where(fold == q, p[E * HEAD :, q * (CW // 4) : (q + 1) * (CW // 4)], rest)
        buf[c, :, :, CW:BW] = rest.reshape(E, HEAD, CW // 4).astype(BF)

    def get(buf, c):
        main = buf[c, :, :, 0:CW].astype(F32).reshape(E * HEAD, CW).astype(BF)
        rest = buf[c, :, :, CW:BW].astype(F32).reshape(E * HEAD, CW // 4)
        rest = jnp.concatenate([jnp.where(fold == q, rest, 0.0) for q in range(4)], axis=1).astype(BF)
        return jnp.concatenate([main, rest], axis=0)

    def own_block(src, dst, c):
        dst[c, me] = src[c, me]

    def send(src, dst, ssem, rsem, c):
        def one(e):
            pltpu.make_async_remote_copy(
                src_ref=src.at[c, e], dst_ref=dst.at[c, me], send_sem=ssem, recv_sem=rsem.at[c],
                device_id=(dp, e), device_id_type=MESH,
            ).start()

        around(one)

    def arrived(buf, rsem, c):
        part = buf.at[c, pl.ds(0, E - 1)]
        pltpu.make_async_copy(part, part, rsem.at[c]).wait()

    def sent(buf, ssem):
        part = buf.at[:, pl.ds(0, E - 1)]
        pltpu.make_async_copy(part, part, ssem).wait()

    def make_v(c):
        w_copy(c).wait()
        put(vs, c, dot(hp[...], wv[c]))
        own_block(vs, vr, c)

    def tell(i):
        r = 2**i
        pl.semaphore_signal(up.at[i], inc=1, device_id=(level(r), me), device_id_type=MESH)
        pl.semaphore_signal(down.at[i], inc=1, device_id=(level(NZ - r), me), device_id_type=MESH)

    def hear(i):
        pl.semaphore_wait(up.at[i], 1)
        pl.semaphore_wait(down.at[i], 1)

    make_v(0)
    pl.semaphore_wait(barrier, 2 * (E - 1) + 3)
    send(vs, vr, vsend, vrecv, 0)

    tell(0)

    def more_v(c):
        make_v(c)
        send(vs, vr, vsend, vrecv, c)

    pl.loop(1, 4)(more_v)
    hear(0)
    tell(1)
    pl.loop(4, NC)(more_v)
    hear(1)
    tell(2)

    for i in range(3):
        small[i].wait()
    ids = idv[...]
    aff = affv[...]
    routed = (iota((E, TOK), 0) == ids).astype(F32)
    before = (iota((TOK, TOK), 0) < iota((TOK, TOK), 1)).astype(F32).astype(BF)
    earlier = dot(routed.astype(BF), before)
    slot = jnp.sum(routed * earlier, axis=0, keepdims=True)
    wanted = slot * float(E) + ids.astype(F32)
    mine = slot_row(iota((ROWS, TOK), 0)).astype(F32) == wanted
    sel[...] = mine.astype(F32)
    total = jnp.sum(aff, axis=0, keepdims=True)
    gate = (ROUTE_SCALE * aff[0:1] / total).astype(BF).astype(F32)

    small[4].wait()
    for j in range(NZ // 2):
        start = 4 * OUT * j
        low = start // 128 * 128
        off = start - low
        width = min(384, D - low) if off + 4 * OUT > 256 else 256
        lane = iota((width, 256), 1)
        source = (2 * ((lane % 128) // HALF) + lane // 128) * OUT + lane % HALF + off
        hot = (iota((width, 256), 0) == source) & (lane % HALF < OUT)
        moved = dot(riv[:, low : low + width], hot.astype(F32).astype(BF)).astype(BF)
        q, h = j // 2, j % 2
        xp[q * TOK : (q + 1) * TOK, h * 128 : (h + 1) * 128] = moved[:, 0:128]
        xp[q * TOK : (q + 1) * TOK, 256 + h * 128 : 256 + (h + 1) * 128] = moved[:, 128:256]

    scaled = (sel[...] * gate).astype(BF)

    @pl.loop(0, NC)
    def _(c):
        og_copy(c).wait()
        put(gs, c, dot(scaled, ogv[c]))
        own_block(gs, gr, c)

    def rows_out(first, last):
        @pl.loop(first, last)
        def _(c):
            send(gs, gr, osend, orecv, c)

    rows_out(0, EARLY)
    hear(2)
    tell(3)

    gsum[...] = jnp.zeros_like(gsum)

    @pl.loop(0, NC)
    def _(c):
        arrived(vr, vrecv, c)
        gsum[...] += dot_t(get(vr, c), ogv[c])

    own = jnp.sum(gsum[...] * sel[...], axis=0, keepdims=True)
    dgate = jnp.concatenate([own, othv[...]], axis=0)
    weighted = jnp.sum(dgate * aff, axis=0, keepdims=True) / total
    grad_logit = ROUTE_SCALE / total * (dgate - weighted) * aff * (1.0 - aff)
    gl_o[...] = grad_logit

    rows = iota((E * 8, TOK), 0)
    picked = jnp.where((rows // 8) == ids, grad_logit[0:1].astype(BF).astype(F32), 0.0)
    wide = jnp.concatenate([jnp.where(rows % 8 == q, picked, 0.0).astype(BF) for q in range(8)], axis=1)
    term = dot(wide, xp[...]).reshape(E, 8, 512).astype(BF)
    p1s[0] = term[:, :, 0:256]
    p1s[1] = term[:, :, 256:512]
    index = core * E + me
    p1r[index] = p1s[core, me]

    def term_to(e, k):
        pltpu.make_async_remote_copy(
            src_ref=p1s.at[k, e], dst_ref=p1r.at[index], send_sem=s1, recv_sem=r1,
            device_id=(z * 2 + k, e), device_id_type=MESH,
        ).start()

    def term_both(e):
        term_to(e, core)
        term_to(e, 1 - core)

    around(term_both)
    term_to(me, 1 - core)
    rows_out(EARLY, NC)

    part = p1r.at[pl.ds(0, 2 * E - 1)]
    pltpu.make_async_copy(part, part, r1).wait()
    plane = jnp.sum(p1r[...].astype(F32), axis=0)
    for q in range(8):
        for h in range(2):
            zs[2 * q + h] = plane[q : q + 1, h * 128 : (h + 1) * 128]
    zr[z] = zs[z // 2]

    hear(3)

    @pl.loop(0, NZ - 1)
    def _(i):
        k = lax.div(i + 1, 2)
        dz = NZ // 2 + k * (1 - 2 * lax.rem(i, 2))
        to = lax.rem(z + dz, NZ)
        pltpu.make_async_remote_copy(
            src_ref=zs.at[lax.div(to, 2)], dst_ref=zr.at[z], send_sem=s2, recv_sem=r2,
            device_id=(to * 2 + core, me), device_id_type=MESH,
        ).start()

    acc[...] = jnp.zeros_like(acc)

    @pl.loop(0, NC)
    def _(c):
        arrived(gr, orecv, c)
        acc[...] += dot_t(get(gr, c), wv[c])

    back = (slot_row(iota((E * CAP, ROWS), 1)) == iota((E * CAP, ROWS), 0)).astype(F32).astype(BF)
    high = acc[...].astype(BF)
    low = (acc[...] - high.astype(F32)).astype(BF)
    gh_o[...] = (dot(back, high) + dot(back, low)).astype(BF)
    sent(vs, vsend)
    sent(gs, osend)

    part = zr.at[pl.ds(0, NZ - 1)]
    pltpu.make_async_copy(part, part, r2).wait()
    column = zr[0]
    for i in range(1, NZ):
        column = column + zr[i]
    gc_o[...] = jnp.where(z % 2 == 0, column[:, 0:OUT], column[:, HALF : HALF + OUT])

    part = p1r.at[pl.ds(0, 2 * E - 1)]
    pltpu.make_async_copy(part, part, s1).wait()
    part = zr.at[pl.ds(0, NZ - 1)]
    pltpu.make_async_copy(part, part, s2).wait()


def body(out_grad, router_input, down_weight, saved_hidden, expert_ids, affinity, other_dgate):
    hidden = saved_hidden[0, 0].transpose(1, 0, 2).reshape(CAP * E, FF)
    vmem, dma = pltpu.VMEM, pltpu.SemaphoreType.DMA
    hbm = pl.BlockSpec(memory_space=pl.ANY)
    here = pl.BlockSpec(memory_space=pltpu.VMEM)
    block = (NC, E, HEAD, BW)
    shapes = (
        jax.ShapeDtypeStruct((CAP * E, FF), BF),
        jax.ShapeDtypeStruct((8, TOK), F32),
        jax.ShapeDtypeStruct((1, OUT), F32),
    )
    results = pl.pallas_call(
        kernel,
        out_shape=tuple(pltpu.VMEM(s.shape, s.dtype) for s in shapes),
        in_specs=[hbm] * 7,
        out_specs=(here, here, here),
        scratch_shapes=[
            vmem((NC, FF, CW), BF), vmem((NC, TOK, CW), BF), vmem((TOK, D), BF), vmem((CAP * E, FF), BF),
            vmem((1, TOK), I32), vmem((8, TOK), F32), vmem((7, TOK), F32),
            vmem((ROWS, FF), BF), vmem((ROWS, TOK), F32), vmem((ROWS, TOK), F32), vmem((ROWS, FF), F32),
            vmem(block, BF), vmem(block, BF), vmem(block, BF), vmem(block, BF),
            vmem((8 * TOK, 512), BF),
            vmem((2, E, 8, 256), BF), vmem((2 * E, 8, 256), BF),
            vmem((NZ // 2, 1, 128), F32), vmem((NZ, 1, 128), F32),
            dma((2 * NC,)), dma((5,)), dma, dma((NC,)), dma, dma((NC,)), dma, dma, dma, dma,
            pltpu.SemaphoreType.REGULAR((4,)), pltpu.SemaphoreType.REGULAR((4,)),
        ],
        compiler_params=pltpu.CompilerParams(
            collective_id=0, has_side_effects=True, vmem_limit_bytes=56 * 1024 * 1024
        ),
    )(out_grad, router_input, down_weight[0], hidden, expert_ids.T, affinity.T, other_dgate.T)
    grad_hidden, grad_logit, grad_centroid = results
    grad_hidden = grad_hidden.reshape(CAP, E, FF).transpose(1, 0, 2)[None, None]
    return grad_hidden, grad_logit.T, grad_centroid


def solution(mesh):
    tokens = P(("dp", "expert"), None)
    slots = P("dp", "expert", None, None, None)
    return jax.shard_map(
        body,
        mesh=mesh,
        in_specs=(tokens, tokens, P("expert", None, None), slots, tokens, tokens, tokens),
        out_specs=(slots, tokens, P("expert", "dp")),
        check_vma=False,
    )
```

```python
import jax
import jax.numpy as jnp
from jax import lax
from jax.experimental import pallas as pl
from jax.experimental.pallas import tpu as pltpu
from jax.sharding import PartitionSpec as P

MESH = pl.DeviceIdType.MESH
ROUTE_SCALE = 2.5
BF = jnp.bfloat16
F32 = jnp.float32
I32 = jnp.int32

SIDE = 4
E = SIDE * SIDE
CAP = 10
HEAD = 8
TOK = 128
D = 3584
FF = 1024
CW = 512
NC = D // CW
BW = CW + CW // 4
ROWS = 2 * E * HEAD
NZ = 32
OUT = 56
HALF = 64
EARLY = 2
MID = 4

_HOP = (0, 1, 2, 1)
_ORDER = sorted(
    [(dx, dy) for dy in range(SIDE) for dx in range(SIDE) if (dx, dy) != (0, 0)],
    key=lambda o: -(_HOP[o[0]] + _HOP[o[1]]),
)


def dot(a, b):
    return jnp.dot(a, b, preferred_element_type=F32)


def dot_t(a, b):
    return lax.dot_general(a, b, (((1,), (1,)), ((), ())), preferred_element_type=F32)


def iota(shape, dim):
    return lax.broadcasted_iota(I32, shape, dim)


def slot_row(i):
    j = i - E * HEAD
    main = (i % HEAD) * E + i // HEAD
    rest = (HEAD + j % 2) * E + j // HEAD
    return jnp.where(i < E * HEAD, main, rest)


def kernel(
    og_h, ri_h, w_h, hid_h, ids_h, aff_h, oth_h,
    gh_o, gl_o, gc_o,
    wv, ogv, riv, hidv, idv, affv, othv,
    hp, sel, gsum, acc, vs, vr, gs, gr, xp, p1s, p1r, zs, zr,
    wsem, lsem, vsend, vrecv, osend, orecv, s1, r1, s2, r2, up, down, pair,
):
    dp = lax.axis_index("dp")
    me = lax.axis_index("expert")
    z, core = lax.div(dp, 2), lax.rem(dp, 2)
    x, y = lax.rem(me, SIDE), lax.div(me, SIDE)

    def at(dx, dy):
        return lax.rem(y + dy, SIDE) * SIDE + lax.rem(x + dx, SIDE)

    def level(dz):
        return lax.rem(z + dz, NZ) * 2 + core

    others = [at(dx, dy) for dx, dy in _ORDER]

    def around(body):
        for e in others:
            body(e)

    small = [
        pltpu.make_async_copy(s, d, lsem.at[i])
        for i, (s, d) in enumerate(((ids_h, idv), (aff_h, affv), (oth_h, othv), (hid_h, hidv), (ri_h, riv)))
    ]
    def w_copy(c):
        return pltpu.make_async_copy(w_h.at[:, pl.ds(c * CW, CW)], wv.at[c], wsem.at[c])

    def og_copy(c):
        return pltpu.make_async_copy(og_h.at[:, pl.ds(c * CW, CW)], ogv.at[c], wsem.at[NC + c])

    small[3].start()
    w_copy(0).start()

    barrier = pltpu.get_barrier_semaphore()
    sibling = z * 2 + 1 - core

    def greet(dp, e):
        pl.semaphore_signal(barrier, inc=1, device_id=(dp, e), device_id_type=MESH)

    for e in others:
        greet(dp, e)
    greet(sibling, me)
    greet(level(1), me)
    greet(level(NZ - 1), me)

    for c in range(1, NC):
        w_copy(c).start()
    for copy in small[:3]:
        copy.start()
    for c in range(NC):
        og_copy(c).start()
    small[4].start()

    small[3].wait()
    place = slot_row(iota((ROWS, E * CAP), 0)) == iota((ROWS, E * CAP), 1)
    hp[...] = dot(place.astype(F32).astype(BF), hidv[...]).astype(BF)

    fold = (iota((E * HEAD, CW // 4), 0) % HEAD) // 2

    def put(buf, c, p):
        buf[c, :, :, 0:CW] = p[0 : E * HEAD].reshape(E, HEAD, CW).astype(BF)
        rest = p[E * HEAD :, 0 : CW // 4]
        for q in range(1, 4):
            rest = jnp.where(fold == q, p[E * HEAD :, q * (CW // 4) : (q + 1) * (CW // 4)], rest)
        buf[c, :, :, CW:BW] = rest.reshape(E, HEAD, CW // 4).astype(BF)

    def get(buf, c):
        main = buf[c, :, :, 0:CW].astype(F32).reshape(E * HEAD, CW).astype(BF)
        rest = buf[c, :, :, CW:BW].astype(F32).reshape(E * HEAD, CW // 4)
        rest = jnp.concatenate([jnp.where(fold == q, rest, 0.0) for q in range(4)], axis=1).astype(BF)
        return jnp.concatenate([main, rest], axis=0)

    def own_block(src, dst, c):
        dst[c, me] = src[c, me]

    def send(src, dst, ssem, rsem, c):
        def one(e):
            pltpu.make_async_remote_copy(
                src_ref=src.at[c, e], dst_ref=dst.at[c, me], send_sem=ssem, recv_sem=rsem.at[c],
                device_id=(dp, e), device_id_type=MESH,
            ).start()

        around(one)

    def arrived(buf, rsem, c):
        part = buf.at[c, pl.ds(0, E - 1)]
        pltpu.make_async_copy(part, part, rsem.at[c]).wait()

    def sent(buf, ssem):
        part = buf.at[:, pl.ds(0, E - 1)]
        pltpu.make_async_copy(part, part, ssem).wait()

    def make_v(c):
        w_copy(c).wait()
        put(vs, c, dot(hp[...], wv[c]))
        own_block(vs, vr, c)

    def tell(i):
        r = 2**i
        pl.semaphore_signal(up.at[i], inc=1, device_id=(level(r), me), device_id_type=MESH)
        pl.semaphore_signal(down.at[i], inc=1, device_id=(level(NZ - r), me), device_id_type=MESH)

    def hear(i):
        pl.semaphore_wait(up.at[i], 1)
        pl.semaphore_wait(down.at[i], 1)

    make_v(0)
    pl.semaphore_wait(barrier, E + 2)
    send(vs, vr, vsend, vrecv, 0)
    pl.semaphore_signal(pair, inc=1, device_id=(sibling, me), device_id_type=MESH)

    tell(0)

    def more_v(c):
        make_v(c)
        send(vs, vr, vsend, vrecv, c)

    pl.loop(1, 4)(more_v)
    hear(0)
    tell(1)
    pl.loop(4, NC)(more_v)
    hear(1)
    tell(2)

    for i in range(3):
        small[i].wait()
    ids = idv[...]
    aff = affv[...]
    routed = (iota((E, TOK), 0) == ids).astype(F32)
    before = (iota((TOK, TOK), 0) < iota((TOK, TOK), 1)).astype(F32).astype(BF)
    earlier = dot(routed.astype(BF), before)
    slot = jnp.sum(routed * earlier, axis=0, keepdims=True)
    wanted = slot * float(E) + ids.astype(F32)
    mine = slot_row(iota((ROWS, TOK), 0)).astype(F32) == wanted
    sel[...] = mine.astype(F32)
    total = jnp.sum(aff, axis=0, keepdims=True)
    gate = (ROUTE_SCALE * aff[0:1] / total).astype(BF).astype(F32)

    small[4].wait()
    for j in range(NZ // 2):
        start = 4 * OUT * j
        low = start // 128 * 128
        off = start - low
        width = min(384, D - low) if off + 4 * OUT > 256 else 256
        lane = iota((width, 256), 1)
        source = (2 * ((lane % 128) // HALF) + lane // 128) * OUT + lane % HALF + off
        hot = (iota((width, 256), 0) == source) & (lane % HALF < OUT)
        moved = dot(riv[:, low : low + width], hot.astype(F32).astype(BF)).astype(BF)
        q, h = j // 2, j % 2
        xp[q * TOK : (q + 1) * TOK, h * 128 : (h + 1) * 128] = moved[:, 0:128]
        xp[q * TOK : (q + 1) * TOK, 256 + h * 128 : 256 + (h + 1) * 128] = moved[:, 128:256]

    scaled = (sel[...] * gate).astype(BF)

    @pl.loop(0, NC)
    def _(c):
        og_copy(c).wait()
        put(gs, c, dot(scaled, ogv[c]))
        own_block(gs, gr, c)

    def rows_out(first, last):
        @pl.loop(first, last)
        def _(c):
            send(gs, gr, osend, orecv, c)

    rows_out(0, EARLY)
    hear(2)
    tell(3)

    gsum[...] = jnp.zeros_like(gsum)

    @pl.loop(0, NC)
    def _(c):
        arrived(vr, vrecv, c)
        gsum[...] += dot_t(get(vr, c), ogv[c])

    own = jnp.sum(gsum[...] * sel[...], axis=0, keepdims=True)
    dgate = jnp.concatenate([own, othv[...]], axis=0)
    weighted = jnp.sum(dgate * aff, axis=0, keepdims=True) / total
    grad_logit = ROUTE_SCALE / total * (dgate - weighted) * aff * (1.0 - aff)
    gl_o[...] = grad_logit

    rows = iota((E * 8, TOK), 0)
    picked = jnp.where((rows // 8) == ids, grad_logit[0:1].astype(BF).astype(F32), 0.0)
    wide = jnp.concatenate([jnp.where(rows % 8 == q, picked, 0.0).astype(BF) for q in range(8)], axis=1)
    term = dot(wide, xp[...]).reshape(E, 8, 512).astype(BF)
    p1s[0] = term[:, :, 0:256]
    p1s[1] = term[:, :, 256:512]
    index = core * E + me
    p1r[index] = p1s[core, me]

    def term_to(e, k):
        pltpu.make_async_remote_copy(
            src_ref=p1s.at[k, e], dst_ref=p1r.at[index], send_sem=s1, recv_sem=r1,
            device_id=(z * 2 + k, e), device_id_type=MESH,
        ).start()

    def term_both(e):
        term_to(e, core)
        term_to(e, 1 - core)

    pl.semaphore_wait(pair, 1)
    around(term_both)
    term_to(me, 1 - core)
    rows_out(EARLY, MID)

    part = p1r.at[pl.ds(0, 2 * E - 1)]
    pltpu.make_async_copy(part, part, r1).wait()
    plane = jnp.sum(p1r[...].astype(F32), axis=0)
    for q in range(8):
        for h in range(2):
            zs[2 * q + h] = plane[q : q + 1, h * 128 : (h + 1) * 128]
    zr[z] = zs[z // 2]

    hear(3)

    @pl.loop(0, NZ - 1)
    def _(i):
        k = lax.div(i + 1, 2)
        dz = NZ // 2 + k * (1 - 2 * lax.rem(i, 2))
        to = lax.rem(z + dz, NZ)
        pltpu.make_async_remote_copy(
            src_ref=zs.at[lax.div(to, 2)], dst_ref=zr.at[z], send_sem=s2, recv_sem=r2,
            device_id=(to * 2 + core, me), device_id_type=MESH,
        ).start()

    rows_out(MID, NC)

    acc[...] = jnp.zeros_like(acc)

    @pl.loop(0, NC)
    def _(c):
        arrived(gr, orecv, c)
        acc[...] += dot_t(get(gr, c), wv[c])

    back = (slot_row(iota((E * CAP, ROWS), 1)) == iota((E * CAP, ROWS), 0)).astype(F32).astype(BF)
    high = acc[...].astype(BF)
    low = (acc[...] - high.astype(F32)).astype(BF)
    gh_o[...] = (dot(back, high) + dot(back, low)).astype(BF)
    sent(vs, vsend)
    sent(gs, osend)

    part = zr.at[pl.ds(0, NZ - 1)]
    pltpu.make_async_copy(part, part, r2).wait()
    column = zr[0]
    for i in range(1, NZ):
        column = column + zr[i]
    gc_o[...] = jnp.where(z % 2 == 0, column[:, 0:OUT], column[:, HALF : HALF + OUT])

    part = p1r.at[pl.ds(0, 2 * E - 1)]
    pltpu.make_async_copy(part, part, s1).wait()
    part = zr.at[pl.ds(0, NZ - 1)]
    pltpu.make_async_copy(part, part, s2).wait()


def hand_over(a, b, c, a_o, b_o, c_o, sem):
    copies = [pltpu.make_async_copy(s, d, sem.at[i]) for i, (s, d) in enumerate(((a, a_o), (b, b_o), (c, c_o)))]
    for copy in copies:
        copy.start()
    for copy in copies:
        copy.wait()


def body(out_grad, router_input, down_weight, saved_hidden, expert_ids, affinity, other_dgate):
    hidden = saved_hidden[0, 0].transpose(1, 0, 2).reshape(CAP * E, FF)
    vmem, dma = pltpu.VMEM, pltpu.SemaphoreType.DMA
    hbm = pl.BlockSpec(memory_space=pl.ANY)
    here = pl.BlockSpec(memory_space=pltpu.VMEM)
    block = (NC, E, HEAD, BW)
    shapes = (
        jax.ShapeDtypeStruct((CAP * E, FF), BF),
        jax.ShapeDtypeStruct((8, TOK), F32),
        jax.ShapeDtypeStruct((1, OUT), F32),
    )
    results = pl.pallas_call(
        kernel,
        out_shape=tuple(pltpu.VMEM(s.shape, s.dtype) for s in shapes),
        in_specs=[hbm] * 7,
        out_specs=(here, here, here),
        scratch_shapes=[
            vmem((NC, FF, CW), BF), vmem((NC, TOK, CW), BF), vmem((TOK, D), BF), vmem((CAP * E, FF), BF),
            vmem((1, TOK), I32), vmem((8, TOK), F32), vmem((7, TOK), F32),
            vmem((ROWS, FF), BF), vmem((ROWS, TOK), F32), vmem((ROWS, TOK), F32), vmem((ROWS, FF), F32),
            vmem(block, BF), vmem(block, BF), vmem(block, BF), vmem(block, BF),
            vmem((8 * TOK, 512), BF),
            vmem((2, E, 8, 256), BF), vmem((2 * E, 8, 256), BF),
            vmem((NZ // 2, 1, 128), F32), vmem((NZ, 1, 128), F32),
            dma((2 * NC,)), dma((5,)), dma, dma((NC,)), dma, dma((NC,)), dma, dma, dma, dma,
            pltpu.SemaphoreType.REGULAR((4,)), pltpu.SemaphoreType.REGULAR((4,)), pltpu.SemaphoreType.REGULAR,
        ],
        compiler_params=pltpu.CompilerParams(
            collective_id=0, has_side_effects=True, vmem_limit_bytes=56 * 1024 * 1024
        ),
    )(out_grad, router_input, down_weight[0], hidden, expert_ids.T, affinity.T, other_dgate.T)
    grad_hidden, grad_logit, grad_centroid = pl.pallas_call(
        hand_over,
        out_shape=shapes,
        in_specs=[here] * 3,
        out_specs=(hbm, hbm, hbm),
        scratch_shapes=[dma((3,))],
    )(*(pltpu.with_memory_space_constraint(a, pltpu.VMEM) for a in results))
    grad_hidden = grad_hidden.reshape(CAP, E, FF).transpose(1, 0, 2)[None, None]
    return grad_hidden, grad_logit.T, grad_centroid


def solution(mesh):
    tokens = P(("dp", "expert"), None)
    slots = P("dp", "expert", None, None, None)
    return jax.shard_map(
        body,
        mesh=mesh,
        in_specs=(tokens, tokens, P("expert", None, None), slots, tokens, tokens, tokens),
        out_specs=(slots, tokens, P("expert", "dp")),
        check_vma=False,
    )
```

```python
import jax
import jax.numpy as jnp
from jax import lax
from jax.experimental import pallas as pl
from jax.experimental.pallas import tpu as pltpu
from jax.sharding import PartitionSpec as P

MESH = pl.DeviceIdType.MESH
ROUTE_SCALE = 2.5
BF = jnp.bfloat16
F32 = jnp.float32
I32 = jnp.int32

SIDE = 4
E = SIDE * SIDE
CAP = 10
HEAD = 8
TOK = 128
D = 3584
FF = 1024
CW = 512
NC = D // CW
BW = CW + CW // 4
ROWS = 2 * E * HEAD
NZ = 32
OUT = 56
HALF = 64
EARLY = 2
MID = 4

_ORDER = (
    (2, 2), (2, 1), (1, 2), (2, 3), (3, 2), (1, 1), (3, 3), (1, 3), (3, 1),
    (2, 0), (0, 2), (1, 0), (0, 1), (3, 0), (0, 3),
)


def dot(a, b):
    return jnp.dot(a, b, preferred_element_type=F32)


def dot_t(a, b):
    return lax.dot_general(a, b, (((1,), (1,)), ((), ())), preferred_element_type=F32)


def iota(shape, dim):
    return lax.broadcasted_iota(I32, shape, dim)


def slot_row(i):
    j = i - E * HEAD
    main = (i % HEAD) * E + i // HEAD
    rest = (HEAD + j % 2) * E + j // HEAD
    return jnp.where(i < E * HEAD, main, rest)


def kernel(
    og_h, ri_h, w_h, hid_h, ids_h, aff_h, oth_h,
    gh_o, gl_o, gc_o,
    wv, ogv, riv, hidv, idv, affv, othv,
    hp, sel, acc, vs, vr, gs, gr, xp, p1s, p1r, zs, zr,
    wsem, lsem, vsend, vrecv, osend, orecv, s1, r1, s2, r2, up, down, pair,
):
    dp = lax.axis_index("dp")
    me = lax.axis_index("expert")
    z, core = lax.div(dp, 2), lax.rem(dp, 2)
    x, y = lax.rem(me, SIDE), lax.div(me, SIDE)

    def at(dx, dy):
        return lax.rem(y + dy, SIDE) * SIDE + lax.rem(x + dx, SIDE)

    def level(dz):
        return lax.rem(z + dz, NZ) * 2 + core

    others = [at(dx, dy) for dx, dy in _ORDER]

    def around(body):
        for e in others:
            body(e)

    small = [
        pltpu.make_async_copy(s, d, lsem.at[i])
        for i, (s, d) in enumerate(((ids_h, idv), (aff_h, affv), (oth_h, othv), (hid_h, hidv), (ri_h, riv)))
    ]
    def w_copy(c):
        return pltpu.make_async_copy(w_h.at[:, pl.ds(c * CW, CW)], wv.at[c], wsem.at[c])

    def og_copy(c):
        return pltpu.make_async_copy(og_h.at[:, pl.ds(c * CW, CW)], ogv.at[c], wsem.at[NC + c])

    small[3].start()
    w_copy(0).start()

    barrier = pltpu.get_barrier_semaphore()
    sibling = z * 2 + 1 - core

    def greet(dp, e):
        pl.semaphore_signal(barrier, inc=1, device_id=(dp, e), device_id_type=MESH)

    for e in others:
        greet(dp, e)
    greet(sibling, me)
    greet(level(1), me)
    greet(level(NZ - 1), me)

    for c in range(1, NC):
        w_copy(c).start()
    for copy in small[:3]:
        copy.start()
    for c in range(NC):
        og_copy(c).start()
    small[4].start()

    small[3].wait()
    place = slot_row(iota((ROWS, E * CAP), 0)) == iota((ROWS, E * CAP), 1)
    hp[...] = dot(place.astype(F32).astype(BF), hidv[...]).astype(BF)

    fold = (iota((E * HEAD, CW // 4), 0) % HEAD) // 2

    def put(buf, c, p):
        buf[c, :, :, 0:CW] = p[0 : E * HEAD].reshape(E, HEAD, CW).astype(BF)
        rest = p[E * HEAD :, 0 : CW // 4]
        for q in range(1, 4):
            rest = jnp.where(fold == q, p[E * HEAD :, q * (CW // 4) : (q + 1) * (CW // 4)], rest)
        buf[c, :, :, CW:BW] = rest.reshape(E, HEAD, CW // 4).astype(BF)

    def get(buf, c):
        main = buf[c, :, :, 0:CW].astype(F32).reshape(E * HEAD, CW).astype(BF)
        rest = buf[c, :, :, CW:BW].astype(F32).reshape(E * HEAD, CW // 4)
        rest = jnp.concatenate([jnp.where(fold == q, rest, 0.0) for q in range(4)], axis=1).astype(BF)
        return jnp.concatenate([main, rest], axis=0)

    def own_block(src, dst, c):
        dst[c, me] = src[c, me]

    def send(src, dst, ssem, rsem, c):
        def one(e):
            pltpu.make_async_remote_copy(
                src_ref=src.at[c, e], dst_ref=dst.at[c, me], send_sem=ssem, recv_sem=rsem.at[c],
                device_id=(dp, e), device_id_type=MESH,
            ).start()

        around(one)

    def arrived(buf, rsem, c):
        part = buf.at[c, pl.ds(0, E - 1)]
        pltpu.make_async_copy(part, part, rsem.at[c]).wait()

    def sent(buf, ssem):
        part = buf.at[:, pl.ds(0, E - 1)]
        pltpu.make_async_copy(part, part, ssem).wait()

    def make_v(c):
        w_copy(c).wait()
        put(vs, c, dot(hp[...], wv[c]))
        own_block(vs, vr, c)

    def tell(i):
        r = 2**i
        pl.semaphore_signal(up.at[i], inc=1, device_id=(level(r), me), device_id_type=MESH)
        pl.semaphore_signal(down.at[i], inc=1, device_id=(level(NZ - r), me), device_id_type=MESH)

    def hear(i):
        pl.semaphore_wait(up.at[i], 1)
        pl.semaphore_wait(down.at[i], 1)

    make_v(0)
    pl.semaphore_wait(barrier, E + 2)
    send(vs, vr, vsend, vrecv, 0)
    pl.semaphore_signal(pair, inc=1, device_id=(sibling, me), device_id_type=MESH)

    tell(0)

    def more_v(c):
        make_v(c)
        send(vs, vr, vsend, vrecv, c)

    pl.loop(1, 4)(more_v)
    hear(0)
    tell(1)
    pl.loop(4, NC)(more_v)
    hear(1)
    tell(2)

    for i in range(3):
        small[i].wait()
    ids = idv[...]
    aff = affv[...]
    routed = (iota((E, TOK), 0) == ids).astype(F32)
    before = (iota((TOK, TOK), 0) < iota((TOK, TOK), 1)).astype(F32).astype(BF)
    earlier = dot(routed.astype(BF), before)
    slot = jnp.sum(routed * earlier, axis=0, keepdims=True)
    wanted = slot * float(E) + ids.astype(F32)
    mine = slot_row(iota((ROWS, TOK), 0)).astype(F32) == wanted
    sel[...] = mine.astype(F32)
    total = jnp.sum(aff, axis=0, keepdims=True)
    gate = (ROUTE_SCALE * aff[0:1] / total).astype(BF).astype(F32)

    small[4].wait()
    for j in range(NZ // 2):
        start = 4 * OUT * j
        low = start // 128 * 128
        off = start - low
        width = min(384, D - low) if off + 4 * OUT > 256 else 256
        lane = iota((width, 256), 1)
        source = (2 * ((lane % 128) // HALF) + lane // 128) * OUT + lane % HALF + off
        hot = (iota((width, 256), 0) == source) & (lane % HALF < OUT)
        moved = dot(riv[:, low : low + width], hot.astype(F32).astype(BF)).astype(BF)
        q, h = j // 2, j % 2
        xp[q * TOK : (q + 1) * TOK, h * 128 : (h + 1) * 128] = moved[:, 0:128]
        xp[q * TOK : (q + 1) * TOK, 256 + h * 128 : 256 + (h + 1) * 128] = moved[:, 128:256]

    scaled = (sel[...] * gate).astype(BF)

    @pl.loop(0, NC)
    def _(c):
        og_copy(c).wait()
        put(gs, c, dot(scaled, ogv[c]))
        own_block(gs, gr, c)

    def rows_out(first, last):
        @pl.loop(first, last)
        def _(c):
            send(gs, gr, osend, orecv, c)

    rows_out(0, EARLY)
    hear(2)
    tell(3)

    def more_own(c, so_far):
        arrived(vr, vrecv, c)
        found = dot_t(get(vr, c), ogv[c]) * sel[...]
        return so_far + jnp.sum(found.reshape(ROWS // 8, 8, TOK), axis=0)

    own = jnp.sum(lax.fori_loop(0, NC, more_own, jnp.zeros((8, TOK), F32)), axis=0, keepdims=True)
    dgate = jnp.concatenate([own, othv[...]], axis=0)
    weighted = jnp.sum(dgate * aff, axis=0, keepdims=True) / total
    grad_logit = ROUTE_SCALE / total * (dgate - weighted) * aff * (1.0 - aff)
    gl_o[...] = grad_logit

    rows = iota((E * 8, TOK), 0)
    picked = jnp.where((rows // 8) == ids, grad_logit[0:1].astype(BF).astype(F32), 0.0)
    wide = jnp.concatenate([jnp.where(rows % 8 == q, picked, 0.0).astype(BF) for q in range(8)], axis=1)
    term = dot(wide, xp[...]).reshape(E, 8, 512).astype(BF)
    p1s[0] = term[:, :, 0:256]
    p1s[1] = term[:, :, 256:512]
    index = core * E + me
    p1r[index] = p1s[core, me]

    def term_to(e, k):
        pltpu.make_async_remote_copy(
            src_ref=p1s.at[k, e], dst_ref=p1r.at[index], send_sem=s1, recv_sem=r1,
            device_id=(z * 2 + k, e), device_id_type=MESH,
        ).start()

    def term_both(e):
        term_to(e, core)
        term_to(e, 1 - core)

    pl.semaphore_wait(pair, 1)
    around(term_both)
    term_to(me, 1 - core)
    rows_out(EARLY, MID)

    part = p1r.at[pl.ds(0, 2 * E - 1)]
    pltpu.make_async_copy(part, part, r1).wait()
    plane = jnp.sum(p1r[...].astype(F32), axis=0)
    for q in range(8):
        for h in range(2):
            zs[2 * q + h] = plane[q : q + 1, h * 128 : (h + 1) * 128]
    zr[z] = zs[z // 2]

    hear(3)

    @pl.loop(0, NZ - 1)
    def _(i):
        k = lax.div(i + 1, 2)
        dz = NZ // 2 + k * (1 - 2 * lax.rem(i, 2))
        to = lax.rem(z + dz, NZ)
        pltpu.make_async_remote_copy(
            src_ref=zs.at[lax.div(to, 2)], dst_ref=zr.at[z], send_sem=s2, recv_sem=r2,
            device_id=(to * 2 + core, me), device_id_type=MESH,
        ).start()

    rows_out(MID, NC)

    acc[...] = jnp.zeros_like(acc)

    @pl.loop(0, NC)
    def _(c):
        arrived(gr, orecv, c)
        acc[...] += dot_t(get(gr, c), wv[c])

    back = (slot_row(iota((E * CAP, ROWS), 1)) == iota((E * CAP, ROWS), 0)).astype(F32).astype(BF)
    high = acc[...].astype(BF)
    low = (acc[...] - high.astype(F32)).astype(BF)
    gh_o[...] = (dot(back, high) + dot(back, low)).astype(BF)
    sent(vs, vsend)
    sent(gs, osend)

    part = zr.at[pl.ds(0, NZ - 1)]
    pltpu.make_async_copy(part, part, r2).wait()
    column = zr[0]
    for i in range(1, NZ):
        column = column + zr[i]
    gc_o[...] = jnp.where(z % 2 == 0, column[:, 0:OUT], column[:, HALF : HALF + OUT])

    part = p1r.at[pl.ds(0, 2 * E - 1)]
    pltpu.make_async_copy(part, part, s1).wait()
    part = zr.at[pl.ds(0, NZ - 1)]
    pltpu.make_async_copy(part, part, s2).wait()


def hand_over(a, b, c, a_o, b_o, c_o, sem):
    copies = [pltpu.make_async_copy(s, d, sem.at[i]) for i, (s, d) in enumerate(((a, a_o), (b, b_o), (c, c_o)))]
    for copy in copies:
        copy.start()
    for copy in copies:
        copy.wait()


def body(out_grad, router_input, down_weight, saved_hidden, expert_ids, affinity, other_dgate):
    hidden = saved_hidden[0, 0].transpose(1, 0, 2).reshape(CAP * E, FF)
    vmem, dma = pltpu.VMEM, pltpu.SemaphoreType.DMA
    hbm = pl.BlockSpec(memory_space=pl.ANY)
    here = pl.BlockSpec(memory_space=pltpu.VMEM)
    block = (NC, E, HEAD, BW)
    shapes = (
        jax.ShapeDtypeStruct((CAP * E, FF), BF),
        jax.ShapeDtypeStruct((8, TOK), F32),
        jax.ShapeDtypeStruct((1, OUT), F32),
    )
    results = pl.pallas_call(
        kernel,
        out_shape=tuple(pltpu.VMEM(s.shape, s.dtype) for s in shapes),
        in_specs=[hbm] * 7,
        out_specs=(here, here, here),
        scratch_shapes=[
            vmem((NC, FF, CW), BF), vmem((NC, TOK, CW), BF), vmem((TOK, D), BF), vmem((CAP * E, FF), BF),
            vmem((1, TOK), I32), vmem((8, TOK), F32), vmem((7, TOK), F32),
            vmem((ROWS, FF), BF), vmem((ROWS, TOK), F32), vmem((ROWS, FF), F32),
            vmem(block, BF), vmem(block, BF), vmem(block, BF), vmem(block, BF),
            vmem((8 * TOK, 512), BF),
            vmem((2, E, 8, 256), BF), vmem((2 * E, 8, 256), BF),
            vmem((NZ // 2, 1, 128), F32), vmem((NZ, 1, 128), F32),
            dma((2 * NC,)), dma((5,)), dma, dma((NC,)), dma, dma((NC,)), dma, dma, dma, dma,
            pltpu.SemaphoreType.REGULAR((4,)), pltpu.SemaphoreType.REGULAR((4,)), pltpu.SemaphoreType.REGULAR,
        ],
        compiler_params=pltpu.CompilerParams(
            collective_id=0, has_side_effects=True, vmem_limit_bytes=56 * 1024 * 1024
        ),
    )(out_grad, router_input, down_weight[0], hidden, expert_ids.T, affinity.T, other_dgate.T)
    grad_hidden, grad_logit, grad_centroid = pl.pallas_call(
        hand_over,
        out_shape=shapes,
        in_specs=[here] * 3,
        out_specs=(hbm, hbm, hbm),
        scratch_shapes=[dma((3,))],
    )(*(pltpu.with_memory_space_constraint(a, pltpu.VMEM) for a in results))
    grad_hidden = grad_hidden.reshape(CAP, E, FF).transpose(1, 0, 2)[None, None]
    return grad_hidden, grad_logit.T, grad_centroid


def solution(mesh):
    tokens = P(("dp", "expert"), None)
    slots = P("dp", "expert", None, None, None)
    return jax.shard_map(
        body,
        mesh=mesh,
        in_specs=(tokens, tokens, P("expert", None, None), slots, tokens, tokens, tokens),
        out_specs=(slots, tokens, P("expert", "dp")),
        check_vma=False,
    )
```
